128 devices in a mesh: row: 16 (over y, x), col: 8 (over z, core).
Axes of the slice: x: 4, y: 4, z: 4, core: 2. Of those that a mesh axis runs over, the one named last changes fastest.
Arguments:
- queries: bfloat16 [2048, 64, 128], P(('row', 'col')), may hold values from -1.75 to 1.75
- passages: bfloat16 [16384, 192, 128], P(('row', 'col')), may hold values from -1.75 to 1.75
- pass_len: int32 [16384], P(('row', 'col')), may hold values from 48 to 192
- send_cont: int32 [128, 128, 4], P(('row', 'col')), may hold values from 0 to 15, as said below
- send_count: int32 [128, 128], P(('row', 'col')), may hold values from 0 to 4, as said below
- cand: int32 [128, 128, 4, 4], P(('row', 'col')), may hold values from 0 to 127
- cand_count: int32 [128, 128, 4], P(('row', 'col')), may hold values from 1 to 4
Outputs:
- scores: float32 [128, 128, 4, 4], P(('row', 'col'))
- best: float32 [2048], P(('row', 'col'))
The draws below stay inside these ranges and needn't reach their ends.
Inputs may be any that keep to these rules, and one draw needn't show every extreme that they name: The 4 entries of send_cont[s, o, :] are distinct. `send_count`: in every draw some owner receives 4 used slots from every device.
All inputs are finite; a program needn't handle non-finite values.
Results may differ from the reference program's by a relative error of at most 0.0003.
Values may be sent and summed in bfloat16 or wider, within the bound.
No kernel may reach another device: no remote copies, remote signals or barrier semaphores. Data moves between devices by JAX's collectives and lax.ppermute only.
A program may use at most 128 MiB of HBM per device.

```python
import jax
import jax.numpy as jnp
from jax import lax

DIM = 128
QL = 64
PL = 192
SLOTS = 4
CAP = 4
Q_DEV = 16
P_DEV = 128
CONT = 2048
NPASS = 16384
DEVICES = 128


def draw_send_cont(key, part):
    key = jax.random.fold_in(key, 11)
    order_key, pick_key, forced_key = jax.random.split(key, 3)
    raw_keys = jax.random.randint(order_key, (DEVICES, DEVICES, Q_DEV), 0, 1 << 20)
    positions = jnp.arange(Q_DEV, dtype=jnp.int32)
    distinct = raw_keys * Q_DEV + positions[None, None, :]
    forced = jax.random.randint(forced_key, (), 0, DEVICES)
    narrow = jax.random.randint(pick_key, (DEVICES,), 0, 8) == 0
    narrow = narrow | (jnp.arange(DEVICES, dtype=jnp.int32) == forced)
    banned = narrow[:, None, None] & (positions[None, None, :] >= Q_DEV // 2)
    distinct = jnp.where(banned, distinct - (1 << 27), distinct)
    picked = jax.lax.top_k(distinct, SLOTS)[1]
    return picked.astype(jnp.int32)


def draw_send_count(key, part):
    key = jax.random.fold_in(key, 12)
    first_key, second_key, third_key = jax.random.split(key, 3)
    hot_owner = jax.random.randint(first_key, (DEVICES,), 0, 4) == 0
    forced = jax.random.randint(second_key, (), 0, DEVICES)
    hot_owner = hot_owner | (jnp.arange(DEVICES, dtype=jnp.int32) == forced)
    base_count = jax.random.randint(third_key, (DEVICES, DEVICES), 0, SLOTS // 2 + 1)
    return jnp.where(hot_owner[None, :], SLOTS, base_count).astype(jnp.int32)


def plant(entries, rng, low, largest):
    dims = entries.shape
    index_at = [jax.random.randint(jax.random.fold_in(rng, axis), (), 0, dims[axis]) for axis in range(len(dims))]
    entries = entries.at[tuple(index_at)].set(low)
    longest = dims.index(max(dims))
    index_at[longest] = (index_at[longest] + 1) % dims[longest]
    return entries.at[tuple(index_at)].set(largest)


def block_levels(own_key, extent, shards, smallest, top_value):
    gain = 1.0
    for axis_at, blocks in shards:
        heights = jax.random.uniform(jax.random.fold_in(jax.random.fold_in(own_key, 6), axis_at), (blocks,), jnp.float32, smallest / len(shards), top_value / len(shards))
        gain = gain * jnp.repeat(jnp.exp(heights), extent[axis_at] // blocks).reshape((-1,) + (1,) * (len(extent) - 1 - axis_at))
    return gain


def centred(own_key, shape, spread, bound, pieces=(), kind=jnp.bfloat16):
    level = block_levels(own_key, shape, pieces, -0.22, 0.18) if pieces else 1.0
    entries = jax.random.normal(own_key, shape, jnp.float32) * spread * level
    return jnp.minimum(jnp.maximum(entries, -bound), bound).astype(kind)


def setup_inputs(seed: int = 0) -> dict:
    seeds = jax.random.split(jax.random.key(seed), 8)
    queries = centred(seeds[0], (CONT, QL, DIM), (DIM ** -0.25), 1.75, ((0, 128),))
    passages = centred(seeds[1], (NPASS, PL, DIM), (DIM ** -0.25), 1.75, ((0, 128),))
    pass_len = plant(jax.random.randint(seeds[2], (NPASS,), PL // 4, PL + 1), jax.random.fold_in(seeds[2], 1), PL // 4, PL).astype(jnp.int32)
    send_cont = draw_send_cont(jax.random.fold_in(seeds[7], 71), 0)
    send_count = draw_send_count(jax.random.fold_in(seeds[7], 71), 0)
    cand = plant(jax.random.randint(seeds[5], (DEVICES, DEVICES, SLOTS, CAP), 0, P_DEV), jax.random.fold_in(seeds[5], 1), 0, P_DEV - 1).astype(jnp.int32)
    cand_count = plant(jax.random.randint(seeds[6], (DEVICES, DEVICES, SLOTS), 1, CAP + 1), jax.random.fold_in(seeds[6], 1), 1, CAP).astype(jnp.int32)
    return {"queries": queries, "passages": passages, "pass_len": pass_len, "send_cont": send_cont, "send_count": send_count, "cand": cand, "cand_count": cand_count}


def score_slots(query_rows, passage_rows, lengths):
    similar = jnp.einsum("sqd,scpd->scqp", query_rows.astype(jnp.float32), passage_rows.astype(jnp.float32))
    inside = jnp.arange(PL, dtype=jnp.int32)[None, None, None, :] < lengths[:, :, None, None]
    column_max = jnp.max(jnp.where(inside, similar, -jnp.inf), axis=3)
    return jnp.mean(column_max, axis=2)


def reference(queries, passages, pass_len, send_cont, send_count, cand, cand_count):
    query_blocks = queries.reshape(DEVICES, Q_DEV, QL, DIM)
    passage_blocks = passages.reshape(DEVICES, P_DEV, PL, DIM)
    length_blocks = pass_len.reshape(DEVICES, P_DEV)

    def per_source(items):
        source_rows, source_slots, source_cands = items

        def per_owner(inner):
            owner, slot_row, cand_row = inner
            owner_vectors = passage_blocks[owner]
            owner_lengths = length_blocks[owner]
            return score_slots(source_rows[slot_row], owner_vectors[cand_row], owner_lengths[cand_row])

        owners = jnp.arange(DEVICES, dtype=jnp.int32)
        return lax.map(per_owner, (owners, source_slots, source_cands))

    raw = lax.map(per_source, (query_blocks, send_cont, cand))
    slot_live = jnp.arange(SLOTS, dtype=jnp.int32)[None, None, :] < send_count[:, :, None]
    cand_live = jnp.arange(CAP, dtype=jnp.int32)[None, None, None, :] < cand_count[:, :, :, None]
    live = slot_live[:, :, :, None] & cand_live
    scores = jnp.where(live, raw, jnp.float32(0.0))
    matches = send_cont[:, :, :, None] == jnp.arange(Q_DEV, dtype=jnp.int32)[None, None, None, :]
    usable = live[:, :, :, :, None] & matches[:, :, :, None, :]
    masked = jnp.where(usable, scores[:, :, :, :, None], -jnp.inf)
    best = jnp.max(masked, axis=(1, 2, 3))
    present = jnp.any(usable, axis=(1, 2, 3))
    best = jnp.where(present, best, jnp.float32(0.0)).reshape(CONT)
    return scores, best
```

```python
import jax
import jax.numpy as jnp
from jax import lax
from jax.experimental import pallas as pl
from jax.experimental.pallas import tpu as pltpu
from jax.sharding import PartitionSpec as P

LANE = 4
UNROLL = 4
MIB = 1 << 20


def smem():
    return pl.BlockSpec(memory_space=pltpu.SMEM)


def vmem():
    return pl.BlockSpec(memory_space=pltpu.VMEM)


def select_kernel(pick, table, out):
    slots = out.shape[0]

    def step(i, carry):
        for k in range(4):
            slot = i * 4 + k
            out[slot] = table[pick[slot]]
        return carry

    lax.fori_loop(0, slots // 4, step, 0)


def select(pick, table):
    shape = (pick.shape[0],) + table.shape[1:]
    return pl.pallas_call(
        select_kernel,
        out_shape=jax.ShapeDtypeStruct(shape, table.dtype),
        in_specs=[smem(), vmem()],
        out_specs=vmem(),
        compiler_params=pltpu.CompilerParams(vmem_limit_bytes=24 * MIB),
    )(pick, table)


def group_kernel(used, cand, group_pass, group_pair, count, filled, latest):
    pairs = cand.shape[0]
    caps = pairs // used.shape[0]

    def clear(i, carry):
        group_pass[i] = 0
        for k in range(LANE):
            group_pair[i * LANE + k] = pairs
        return carry

    lax.fori_loop(0, group_pass.shape[0], clear, 0)

    def clear_passage(i, carry):
        filled[i] = 0
        latest[i] = 0
        return carry

    lax.fori_loop(0, filled.shape[0], clear_passage, 0)

    def slot_step(slot, groups):
        def pair_step(k, groups):
            pair = slot * caps + k
            passage = cand[pair]
            have = filled[passage]
            place = have & (LANE - 1)
            fresh = (place == 0).astype(jnp.int32)
            group = jnp.where(place == 0, groups, latest[passage])
            latest[passage] = group
            filled[passage] = have + 1
            group_pass[group] = passage
            group_pair[group * LANE + place] = pair
            return groups + fresh

        return lax.fori_loop(0, used[slot], pair_step, groups)

    count[0] = lax.fori_loop(0, used.shape[0], slot_step, jnp.int32(0))


def group_pairs(used, cand, passages):
    most = (cand.shape[0] + (LANE - 1) * passages) // LANE
    most = -(-most // UNROLL) * UNROLL
    return pl.pallas_call(
        group_kernel,
        out_shape=(
            jax.ShapeDtypeStruct((most,), jnp.int32),
            jax.ShapeDtypeStruct((most * LANE,), jnp.int32),
            jax.ShapeDtypeStruct((1,), jnp.int32),
        ),
        in_specs=[smem(), smem()],
        out_specs=(smem(), smem(), smem()),
        scratch_shapes=[
            pltpu.SMEM((passages,), jnp.int32),
            pltpu.SMEM((passages,), jnp.int32),
        ],
    )(used, cand)


def score_kernel(group_pass, group_pair, count, rows, passages, out, peaks):
    slots, tokens, width = rows.shape
    pairs = out.shape[1]
    caps = pairs // slots
    peaks[...] = jnp.zeros_like(peaks)
    lower = lax.broadcasted_iota(jnp.int32, (1, 2 * tokens), 1) < tokens

    def step(i, carry):
        for u in range(UNROLL):
            group = i * UNROLL + u
            pair = [group_pair[group * LANE + k] for k in range(LANE)]
            picked = [rows[jnp.minimum(p // caps, slots - 1)] for p in pair]
            similar = lax.dot_general(
                passages[group_pass[group]],
                jnp.concatenate(picked, axis=0),
                (((1,), (1,)), ((), ())),
                preferred_element_type=jnp.float32,
            )
            top = jnp.max(similar, axis=0, keepdims=True)
            for k in range(0, LANE, 2):
                both = top[:, k * tokens : (k + 2) * tokens]
                peaks[pl.ds(pair[k], 1), :] = jnp.where(lower, both, 0.0)
                peaks[pl.ds(pair[k + 1], 1), :] = jnp.where(lower, 0.0, both)
        return carry

    steps = (count[0] + UNROLL - 1) // UNROLL
    lax.fori_loop(0, steps, step, 0)
    total = lax.dot_general(
        jnp.ones((8, 2 * tokens), jnp.float32),
        peaks[0:pairs, :],
        (((1,), (1,)), ((), ())),
        precision=lax.Precision.HIGHEST,
        preferred_element_type=jnp.float32,
    )
    out[...] = total[0:1] * (1.0 / tokens)


def score(groups, rows, passages):
    slots, tokens, width = rows.shape
    pairs = slots * 4
    return pl.pallas_call(
        score_kernel,
        out_shape=jax.ShapeDtypeStruct((1, pairs), jnp.float32),
        in_specs=[smem(), smem(), smem(), vmem(), vmem()],
        out_specs=vmem(),
        scratch_shapes=[pltpu.VMEM((pairs + 8, 2 * tokens), jnp.float32)],
        compiler_params=pltpu.CompilerParams(vmem_limit_bytes=40 * MIB),
    )(*groups, rows, passages)


def body(queries, passages, pass_len, send_cont, send_count, cand, cand_count):
    slot_list = send_cont[0]
    devices, slots = slot_list.shape
    caps = cand.shape[3]
    axes = ("row", "col")

    used = jnp.where(jnp.arange(slots)[None, :] < send_count[0][:, None], cand_count[0], 0)
    notes = jnp.concatenate([used, cand[0].reshape(devices, slots * caps)], axis=1)
    notes = lax.all_to_all(notes, axes, split_axis=0, concat_axis=0, tiled=True)
    outgoing = select(slot_list.reshape(-1), queries)
    outgoing = outgoing.reshape((devices, slots) + queries.shape[1:])
    rows = lax.all_to_all(outgoing, axes, split_axis=0, concat_axis=0, tiled=True)
    rows = rows.reshape((devices * slots,) + queries.shape[1:])

    tokens = lax.broadcasted_iota(jnp.int32, passages.shape[:2], 1)
    inside = tokens < pass_len[:, None]
    filled = jnp.where(inside[:, :, None], passages, passages[:, :1, :])
    groups = group_pairs(
        notes[:, :slots].reshape(-1), notes[:, slots:].reshape(-1), passages.shape[0]
    )
    handled = score(groups, rows, filled).reshape(devices, slots, caps)
    returned = lax.all_to_all(handled, axes, split_axis=0, concat_axis=0, tiled=True)

    live = jnp.arange(caps)[None, None, :] < used[:, :, None]
    scores = jnp.where(live, returned, 0.0)
    conts = jnp.arange(queries.shape[0])
    usable = live[:, :, :, None] & (slot_list[:, :, None] == conts)[:, :, None, :]
    best = jnp.max(jnp.where(usable, scores[:, :, :, None], -jnp.inf), axis=(0, 1, 2))
    best = jnp.where(jnp.any(usable, axis=(0, 1, 2)), best, 0.0)
    return scores[None], best


def solution(mesh):
    both = ("row", "col")
    in_specs = (
        P(both, None, None),
        P(both, None, None),
        P(both),
        P(both, None, None),
        P(both, None),
        P(both, None, None, None),
        P(both, None, None),
    )
    out_specs = (P(both, None, None, None), P(both))
    return jax.shard_map(body, mesh=mesh, in_specs=in_specs, out_specs=out_specs, check_vma=False)
```

```python
import itertools

import jax
import jax.numpy as jnp
from jax import lax
from jax.experimental import pallas as pl
from jax.experimental.pallas import tpu as pltpu
from jax.sharding import Mesh, PartitionSpec as P

ALL = ("y", "x", "z", "core")
PLACE = ("y", "x", "z")
SIDE = 4
CHIPS = SIDE**3
EARLY = CHIPS * 3 // 4
CAPS = 4
SLOTS = 4
LANE = 4
UNROLL = 16
MIB = 1 << 20
CONTS = 16
NOTE_ROWS = 16
NOTES = 128

ORDERS = (("x", "y", "z"), ("y", "z", "x"))


def smem():
    return pl.BlockSpec(memory_space=pltpu.SMEM)


def vmem():
    return pl.BlockSpec(memory_space=pltpu.VMEM)


def hbm():
    return pl.BlockSpec(memory_space=pl.ANY)


def shift(array, stage, by):
    pairs = []
    for y, x, z, core in itertools.product(range(SIDE), range(SIDE), range(SIDE), range(2)):
        at = {"y": y, "x": x, "z": z}
        axis = ORDERS[core][stage]
        to = dict(at, **{axis: (at[axis] + by) % SIDE})
        pairs.append(tuple(((p["y"] * SIDE + p["x"]) * SIDE + p["z"]) * 2 + core for p in (at, to)))
    return lax.ppermute(array, ALL, pairs)


def cost(us):
    return pl.CostEstimate(flops=0, bytes_accessed=int(us * 3_500_000), transcendentals=0)


def chip_low(at, low):
    y, x, z = ((at[k] - low[k]) & (SIDE - 1) for k in "yxz")
    return (y * SIDE + x) * SIDE + z


def by_core(core, digits):
    low = [dict(zip(order, digits)) for order in ORDERS]
    return {k: jnp.where(core == 0, low[0][k], low[1][k]) for k in "yxz"}


def select_kernel(targets, here, after, *refs):
    planes, outs = refs[:SIDE], refs[SIDE : SIDE + len(targets)]
    table, notes, arrived = refs[SIDE + len(targets) :]
    at, core = dict(zip("yxz", (here[0], here[1], here[2]))), here[3]
    end = planes[0].shape[1] - NOTE_ROWS
    tokens = end // CONTS
    for source in range(SIDE * SIDE):
        told = planes[source // SIDE][source % SIDE, end : end + NOTE_ROWS, :]
        table[source] = told.astype(jnp.float32).astype(jnp.int32)[:8]
    copy = pltpu.make_async_copy(table, notes, arrived)
    copy.start()
    owners = []
    for third in targets:
        chip = chip_low(at, by_core(core, (0, 0, -third)))
        owners += [(chip * 2 + core) * SLOTS, (chip * 2 + 1 - core) * SLOTS]
    copy.wait()
    for second in range(SIDE):

        def step(first, carry):
            source = second * SIDE + first
            for out, target in enumerate(outs):
                for slot in range(2 * SLOTS):
                    start = owners[out * 2 + slot // SLOTS]
                    cont = notes[source, start >> 7, (start & 127) + slot % SLOTS]
                    rows = pl.ds(pl.multiple_of(cont * tokens, 16), tokens)
                    target[source * 2 * SLOTS + slot] = planes[second][first, rows, :]
            return carry

        lax.fori_loop(0, SIDE, step, 0)


def select(targets, here, after, planes):
    tokens = (planes[0].shape[1] - NOTE_ROWS) // CONTS
    shape = (SIDE * SIDE * 2 * SLOTS, tokens, planes[0].shape[2])
    return pl.pallas_call(
        lambda *refs: select_kernel(targets, *refs),
        out_shape=[jax.ShapeDtypeStruct(shape, planes[0].dtype)] * len(targets),
        in_specs=[smem(), hbm()] + [vmem()] * SIDE,
        out_specs=[vmem()] * len(targets),
        cost_estimate=cost(4),
        scratch_shapes=[
            pltpu.VMEM((SIDE * SIDE, 8, 128), jnp.int32),
            pltpu.SMEM((SIDE * SIDE, 8, 128), jnp.int32),
            pltpu.SemaphoreType.DMA(()),
        ],
        compiler_params=pltpu.CompilerParams(vmem_limit_bytes=8 * MIB),
    )(here, after, *planes)


def group_kernel(here, notes, after, *refs):
    parts, states = refs[:2], refs[2:]
    nobody = CHIPS * 2 * SLOTS * CAPS
    size = parts[0].shape[0] // 2
    most = (size - 1) // (LANE + 1)
    passages = states[0].shape[0] - 8
    at, core = dict(zip("yxz", (here[0], here[1], here[2]))), here[3]

    def clear(i, carry):
        for u in range(4):
            for groups in parts:
                for start in (0, size):
                    groups[start + most * LANE + i * 4 + u] = 0
                    for k in range(LANE):
                        groups[start + (i * 4 + u) * LANE + k] = nobody
        return carry

    lax.fori_loop(0, most // 4, clear, 0)

    def clear_passage(i, carry):
        for u in range(4):
            for state in states:
                state[i * 4 + u] = 0
        return carry

    lax.fori_loop(0, states[0].shape[0] // 4, clear_passage, 0)

    def sources(first, last, part, ends):
        def source_step(source, ends):
            third = source // (SIDE * SIDE)
            third = third + (third == 2).astype(jnp.int32) - (third == 3).astype(jnp.int32)
            digits = (source % SIDE, source // SIDE % SIDE, third)
            chip = chip_low(at, by_core(core, digits))
            base = chip * NOTES
            ends = list(ends)
            row = chip * (2 * SLOTS * CAPS)
            code = ((source - first) * 2 * SLOTS << 12) | row
            for j in range(SLOTS):
                for which in range(2):
                    groups, state = parts[part], states[part * 2 + which]
                    info = base + which * SLOTS * (1 + CAPS)
                    used = notes[info + j]
                    for k in range(CAPS):
                        slot = which * SLOTS + j
                        passage = notes[info + SLOTS + j * CAPS + k]
                        live = k < used
                        at_state = jnp.where(live, passage, passages)
                        spot = state[at_state]
                        fresh = (spot & (LANE - 1)) == 0
                        spot = jnp.where(fresh, ends[which], spot)
                        state[at_state] = spot + 1
                        spot = jnp.where(live, spot, (most - 1) * LANE)
                        groups[which * size + most * LANE + (spot >> 2)] = passage
                        groups[which * size + spot] = code + ((slot << 12) | (slot * CAPS + k))
                        ends[which] = jnp.where(live & fresh, ends[which] + LANE, ends[which])
            return tuple(ends)

        return lax.fori_loop(first, last, source_step, ends)

    zero = jnp.int32(0)
    for part, (first, last) in enumerate(((0, EARLY), (EARLY, CHIPS))):
        ends = sources(first, last, part, (zero, zero))
        for which in range(2):
            parts[part][which * size + most * (LANE + 1)] = ends[which] // LANE


def group_pairs(here, notes, after, passages):
    most = (EARLY * SLOTS * CAPS + (LANE - 1) * passages) // LANE
    most = (most // UNROLL + 2) * UNROLL
    return pl.pallas_call(
        group_kernel,
        out_shape=[jax.ShapeDtypeStruct((2 * (most * (LANE + 1) + 1),), jnp.int32)] * 2,
        in_specs=[smem(), smem(), hbm()],
        out_specs=[smem()] * 2,
        scratch_shapes=[pltpu.SMEM((passages + 8,), jnp.int32)] * 4,
        cost_estimate=cost(10),
    )(here, notes, after)


def score_kernel(many, groups, lengths, *refs):
    pieces, refs = refs[:many], refs[many:]
    own, sibling, refs = refs[0], refs[1], refs[2:]
    if many > 1:
        out, rows, arrived, peaks = refs
        each = pieces[0].shape[0]
        copies = [
            pltpu.make_async_copy(piece, rows.at[pl.ds(i * each, each)], arrived.at[i])
            for i, piece in enumerate(pieces)
        ]
        for copy in copies:
            copy.start()
        peaks[...] = jnp.zeros_like(peaks)
        for copy in copies:
            copy.wait()
    else:
        before, out, peaks = refs
        rows = pieces[0]
        peaks[...] = jnp.zeros_like(peaks)

    size = groups.shape[0] // 2
    most = (size - 1) // (LANE + 1)
    tokens = rows.shape[1]
    pairs = peaks.shape[0] - 8
    lower = lax.broadcasted_iota(jnp.int32, (1, 2 * tokens), 1) < tokens
    token = lax.broadcasted_iota(jnp.int32, (own.shape[1], LANE * tokens), 0)
    for which, texts in enumerate((own, sibling)):
        start = which * size

        def step(i, carry):
            for u in range(UNROLL):
                group = i * UNROLL + u
                code = [groups[start + group * LANE + k] for k in range(LANE)]
                passage = groups[start + most * LANE + group]
                similar = lax.dot_general(
                    texts[passage],
                    jnp.concatenate([rows[c >> 12] for c in code], axis=0),
                    (((1,), (1,)), ((), ())),
                    preferred_element_type=jnp.float32,
                )
                inside = token < lengths[which * own.shape[0] + passage]
                top = jnp.max(jnp.where(inside, similar, -jnp.inf), axis=0, keepdims=True)
                for k in range(0, LANE, 2):
                    both = top[:, k * tokens : (k + 2) * tokens]
                    peaks[pl.ds(code[k] & 4095, 1), :] = jnp.where(lower, both, 0.0)
                    peaks[pl.ds(code[k + 1] & 4095, 1), :] = jnp.where(lower, 0.0, both)
            return carry

        steps = (groups[start + most * (LANE + 1)] + UNROLL - 1) // UNROLL
        lax.fori_loop(0, steps, step, 0)
    high = peaks[0:pairs, :].astype(jnp.bfloat16)
    low = (peaks[0:pairs, :] - high.astype(jnp.float32)).astype(jnp.bfloat16)
    ones = jnp.ones((16, 2 * tokens), jnp.bfloat16)
    total = sum(
        lax.dot_general(
            ones, part, (((1,), (1,)), ((), ())), preferred_element_type=jnp.float32
        )
        for part in (high, low)
    )
    total = total[0:1] * (1.0 / tokens)
    each = out.shape[1]
    for chip in range(CHIPS):
        out[chip : chip + 1, :] = total[:, chip * each : (chip + 1) * each]
    if many == 1:
        out[...] = out[...] + before[...]


def score(groups, lengths, pieces, own, sibling, before=()):
    pairs = CHIPS * 2 * SLOTS * CAPS
    many = len(pieces)
    tokens = pieces[0].shape[1]
    scratch = [pltpu.VMEM((pairs + 8, 2 * tokens), jnp.float32)]
    if many > 1:
        scratch = [
            pltpu.VMEM((many * pieces[0].shape[0],) + pieces[0].shape[1:], own.dtype),
            pltpu.SemaphoreType.DMA((many,)),
        ] + scratch
    return pl.pallas_call(
        lambda *refs: score_kernel(many, *refs),
        out_shape=jax.ShapeDtypeStruct((CHIPS, pairs // CHIPS), jnp.float32),
        in_specs=[smem()] * 2
        + [hbm() if many > 1 else vmem()] * many
        + [vmem()] * (2 + len(before)),
        out_specs=vmem(),
        scratch_shapes=scratch,
        cost_estimate=cost(12 if many > 1 else 8),
        compiler_params=pltpu.CompilerParams(vmem_limit_bytes=16 * MIB),
    )(groups, lengths, *pieces, own, sibling, *before)


def body(queries, passages, pass_len, send_cont, send_count, cand, cand_count):
    slot_list = send_cont[0]
    devices, slots = slot_list.shape
    caps = cand.shape[3]
    core = lax.axis_index("core")
    here = jnp.stack([lax.axis_index(k) for k in ALL]).astype(jnp.int32)

    used = jnp.where(jnp.arange(slots)[None, :] < send_count[0][:, None], cand_count[0], 0)
    info = jnp.concatenate([used, cand[0].reshape(devices, slots * caps)], axis=1)
    info = info.reshape(CHIPS, 2, -1)
    info = jnp.where(core == 0, info, info[:, ::-1]).reshape(CHIPS, -1)
    info = jnp.pad(info, ((0, 0), (0, NOTES - info.shape[1])))

    told = slot_list.astype(queries.dtype).reshape(-1, 128)
    told = jnp.pad(told, ((0, NOTE_ROWS - told.shape[0]), (0, 0)))
    piece = jnp.concatenate([queries.reshape(-1, queries.shape[2]), told], axis=0)
    line = jnp.stack([piece] + [shift(piece, 0, by) for by in range(1, SIDE)])
    planes = [line] + [shift(line, 1, by) for by in range(1, SIDE)]
    info, _ = lax.optimization_barrier((info, line))
    notes = lax.all_to_all(info, PLACE, split_axis=0, concat_axis=0, tiled=True)

    swap = [(0, 1), (1, 0)]
    sibling = lax.ppermute(passages, "core", swap)
    lengths = jnp.concatenate([pass_len, lax.ppermute(pass_len, "core", swap)])

    up, down = select((1, 3), here, notes, planes)
    near, back = shift(up, 2, 1), shift(down, 2, 3)
    across, here_rows = select((2, 0), here, up, planes)
    early, late = group_pairs(here, notes.reshape(-1), here_rows, passages.shape[0])
    across, early = lax.optimization_barrier((across, early))
    far = shift(across, 2, 2)
    handled = score(early, lengths, [here_rows, near, back], passages, sibling)
    handled = score(late, lengths, [far], passages, sibling, (handled,))
    returned = lax.all_to_all(handled, PLACE, split_axis=0, concat_axis=0, tiled=True)
    returned = returned.reshape(CHIPS, 2, -1)
    returned = jnp.where(core == 0, returned, returned[:, ::-1])
    returned = returned.reshape(devices, slots, caps)

    live = jnp.arange(caps)[None, None, :] < used[:, :, None]
    scores = jnp.where(live, returned, 0.0)
    conts = jnp.arange(queries.shape[0])
    usable = live[:, :, :, None] & (slot_list[:, :, None] == conts)[:, :, None, :]
    best = jnp.max(jnp.where(usable, scores[:, :, :, None], -jnp.inf), axis=(0, 1, 2))
    best = jnp.where(jnp.any(usable, axis=(0, 1, 2)), best, 0.0)
    return scores[None], best


def solution(mesh):
    mesh = Mesh(mesh.devices.reshape(SIDE, SIDE, SIDE, 2), ALL)
    in_specs = (
        P(ALL, None, None),
        P(ALL, None, None),
        P(ALL),
        P(ALL, None, None),
        P(ALL, None),
        P(ALL, None, None, None),
        P(ALL, None, None),
    )
    out_specs = (P(ALL, None, None, None), P(ALL))
    return jax.shard_map(body, mesh=mesh, in_specs=in_specs, out_specs=out_specs, check_vma=False)
```

```python
import itertools

import jax
import jax.numpy as jnp
from jax import lax
from jax.experimental import pallas as pl
from jax.experimental.pallas import tpu as pltpu
from jax.sharding import Mesh, PartitionSpec as P

ALL = ("y", "x", "z", "core")
PLACE = ("y", "x", "z")
SIDE = 4
CHIPS = SIDE**3
EARLY = CHIPS * 3 // 4
CAPS = 4
SLOTS = 4
LANE = 4
UNROLL = 16
NOBODY = EARLY * 2 * SLOTS * CAPS
MIB = 1 << 20
CONTS = 16
NOTE_ROWS = 16
NOTES = 32
PASSAGES = 128

ORDERS = (("x", "y", "z"), ("y", "z", "x"))


def smem():
    return pl.BlockSpec(memory_space=pltpu.SMEM)


def vmem():
    return pl.BlockSpec(memory_space=pltpu.VMEM)


def hbm():
    return pl.BlockSpec(memory_space=pl.ANY)


def shift(array, stage, by):
    pairs = []
    for y, x, z, core in itertools.product(range(SIDE), range(SIDE), range(SIDE), range(2)):
        at = {"y": y, "x": x, "z": z}
        axis = ORDERS[core][stage]
        to = dict(at, **{axis: (at[axis] + by) % SIDE})
        pairs.append(tuple(((p["y"] * SIDE + p["x"]) * SIDE + p["z"]) * 2 + core for p in (at, to)))
    return lax.ppermute(array, ALL, pairs)


def cost(us):
    return pl.CostEstimate(flops=0, bytes_accessed=int(us * 3_500_000), transcendentals=0)


def chip_low(at, low):
    y, x, z = ((at[k] - low[k]) & (SIDE - 1) for k in "yxz")
    return (y * SIDE + x) * SIDE + z


def by_core(core, digits):
    low = [dict(zip(order, digits)) for order in ORDERS]
    return {k: jnp.where(core == 0, low[0][k], low[1][k]) for k in "yxz"}


def select_kernel(targets, here, after, *refs):
    *planes, table, notes, arrived = refs
    planes, outs = planes[: -len(targets)], planes[-len(targets) :]
    at, core = dict(zip("yxz", (here[0], here[1], here[2]))), here[3]
    end = planes[0].shape[1] - NOTE_ROWS
    tokens = end // CONTS
    for source in range(SIDE * len(planes)):
        told = planes[source // SIDE][source % SIDE, end : end + NOTE_ROWS, :]
        table[source] = told.astype(jnp.float32).astype(jnp.int32)[:8]
    copy = pltpu.make_async_copy(table, notes, arrived)
    copy.start()
    owners = []
    for third in targets:
        chip = chip_low(at, by_core(core, (0, 0, -third)))
        owners += [chip * 2 + core, chip * 2 + 1 - core]
    copy.wait()
    for second in range(len(planes)):

        def step(first, carry):
            source = second * SIDE + first
            for out, target in enumerate(outs):
                picked = []
                for slot in range(2 * SLOTS):
                    cont = notes[source, slot % SLOTS, owners[out * 2 + slot // SLOTS]]
                    rows = pl.ds(pl.multiple_of(cont * tokens, 16), tokens)
                    picked.append(planes[second][first, rows, :])
                for slot, rows in enumerate(picked):
                    target[source * 2 * SLOTS + slot] = rows
            return carry

        lax.fori_loop(0, SIDE, step, 0)


def select(targets, here, after, planes):
    tokens = (planes[0].shape[1] - NOTE_ROWS) // CONTS
    sources = SIDE * len(planes)
    shape = (sources * 2 * SLOTS, tokens, planes[0].shape[2])
    return pl.pallas_call(
        lambda *refs: select_kernel(targets, *refs),
        out_shape=[jax.ShapeDtypeStruct(shape, planes[0].dtype)] * len(targets),
        in_specs=[smem(), hbm()] + [vmem()] * len(planes),
        out_specs=[vmem()] * len(targets),
        cost_estimate=cost(4),
        scratch_shapes=[
            pltpu.VMEM((sources, 8, 128), jnp.int32),
            pltpu.SMEM((sources, 8, 128), jnp.int32),
            pltpu.SemaphoreType.DMA(()),
        ],
        compiler_params=pltpu.CompilerParams(vmem_limit_bytes=14 * MIB),
    )(here, after, *planes)


def room(part):
    sources = (EARLY, CHIPS - EARLY)[part]
    most = (sources * SLOTS * CAPS + (LANE - 1) * PASSAGES) // LANE
    return -(-most // 32) * 32


def start_of(part, which):
    before = 2 * sum(room(p) for p in range(part))
    return (before + (room(part) * which if which else 0)) * LANE


def group_kernel(here, notes, held, lists, passed, blank, table, spots, arrived):
    rows, lanes = lists.shape
    counts_row = rows - 8
    dump = counts_row * lanes + lanes // 2
    core = here[3]
    source = lax.broadcasted_iota(jnp.int32, (CHIPS, 1), 0)
    far_y = (here[0] - (source >> 4)) & (SIDE - 1)
    far_x = (here[1] - (source >> 2)) & (SIDE - 1)
    far_z = (here[2] - source) & (SIDE - 1)
    first = jnp.where(core == 0, far_x, far_y)
    second = jnp.where(core == 0, far_y, far_z)
    third = jnp.where(core == 0, far_z, far_x)
    late = third == 2
    third = jnp.where(late, 0, jnp.where(third == 3, 2, third))
    local = (third * SIDE + second) * SIDE + first
    shift_late = jnp.where(late, PASSAGES, 0)

    lane = lax.broadcasted_iota(jnp.int32, (CHIPS, lanes), 1)
    key = lax.broadcasted_iota(jnp.int32, (CHIPS, 2 * PASSAGES), 1)
    square = (CHIPS, CHIPS)
    earlier = lax.broadcasted_iota(jnp.int32, square, 1) < lax.broadcasted_iota(jnp.int32, square, 0)
    earlier = earlier.astype(jnp.float32).astype(jnp.bfloat16)
    square = (PASSAGES, PASSAGES)
    below = lax.broadcasted_iota(jnp.int32, square, 0) < lax.broadcasted_iota(jnp.int32, square, 1)
    below = below.astype(jnp.float32).astype(jnp.bfloat16)
    data = notes[...]
    found = jnp.zeros((CHIPS, lanes), jnp.int32)
    counts = jnp.zeros((1, lanes), jnp.int32)
    lane_row = lax.broadcasted_iota(jnp.int32, (1, lanes), 1)

    for which in range(2):
        info = which * NOTES
        hits, ranks, lives = [], [], []
        many = jnp.zeros((1, 2 * PASSAGES), jnp.float32)
        for j in range(SLOTS):
            for k in range(CAPS):
                at = info + SLOTS + j * CAPS + k
                passage = data[:, at : at + 1]
                live = data[:, info + j : info + j + 1] > k
                hit = jnp.where(live & (passage + shift_late == key), 1.0, 0.0)
                ahead = jnp.dot(
                    earlier, hit.astype(jnp.bfloat16), preferred_element_type=jnp.float32
                )
                ranks.append(jnp.sum(hit * (ahead + many), axis=1, keepdims=True))
                many = many + jnp.sum(hit, axis=0, keepdims=True)
                hits.append(hit)
                lives.append(live)
                slot = local * (2 * SLOTS) + which * SLOTS + j
                code = (passage << 20) | (slot << 11) | (slot * CAPS + k)
                pair = (which * SLOTS + j) * CAPS + k
                found = jnp.where(lane == 32 + pair, code, found)
        groups = (many.astype(jnp.int32) + (LANE - 1)) // LANE
        starts = []
        for part in range(2):
            mine = groups[:, part * PASSAGES : (part + 1) * PASSAGES]
            wide = jnp.broadcast_to(mine.astype(jnp.float32), (16, PASSAGES)).astype(jnp.bfloat16)
            base = jnp.dot(wide, below, preferred_element_type=jnp.float32)[0:1]
            starts.append(base * LANE + start_of(part, which))
            total = jnp.sum(mine.astype(jnp.float32), axis=1, keepdims=True).astype(jnp.int32)
            counts = jnp.where(lane_row == part * 2 + which, total, counts)
        begin = jnp.concatenate(starts, axis=1)
        for i, (hit, rank, live) in enumerate(zip(hits, ranks, lives)):
            spot = jnp.sum(hit * begin, axis=1, keepdims=True) + rank
            spot = jnp.where(live, spot.astype(jnp.int32), dump)
            found = jnp.where(lane == which * SLOTS * CAPS + i, spot, found)

    table[...] = found
    blank[...] = jnp.full((rows, lanes), NOBODY, jnp.int32)
    blank[counts_row : counts_row + 1, :] = counts
    copies = [
        pltpu.make_async_copy(table, spots, arrived.at[0]),
        pltpu.make_async_copy(blank, lists, arrived.at[1]),
    ]
    for copy in copies:
        copy.start()
    for copy in copies:
        copy.wait()

    def scatter(source, carry):
        for pair in range(2 * SLOTS * CAPS):
            spot = spots[source, pair]
            lists[spot >> 7, spot & 127] = spots[source, 32 + pair]
        return carry

    lax.fori_loop(0, CHIPS, scatter, 0)


def group_pairs(here, notes, held):
    rows = start_of(2, 0) // 128 + 8
    rows = -(-rows // 8) * 8
    return pl.pallas_call(
        group_kernel,
        out_shape=(
            jax.ShapeDtypeStruct((rows, 128), jnp.int32),
            jax.ShapeDtypeStruct(held.shape, held.dtype),
        ),
        in_specs=[smem(), vmem(), hbm()],
        out_specs=(smem(), hbm()),
        input_output_aliases={2: 1},
        scratch_shapes=[
            pltpu.VMEM((rows, 128), jnp.int32),
            pltpu.VMEM((CHIPS, 128), jnp.int32),
            pltpu.SMEM((CHIPS, 128), jnp.int32),
            pltpu.SemaphoreType.DMA((2,)),
        ],
        cost_estimate=cost(8),
        compiler_params=pltpu.CompilerParams(vmem_limit_bytes=16 * MIB),
    )(here, notes, held)


def score_kernel(part, many, here, lists, lengths, *refs):
    pieces, refs = refs[:many], refs[many:]
    own, sibling, refs = refs[0], refs[1], refs[2:]
    *refs, theirs, arrived, peaks = refs
    swap_in = pltpu.make_async_copy(sibling, theirs, arrived.at[many])
    *before, out, rows = refs
    each = pieces[0].shape[0]
    copies = [
        pltpu.make_async_copy(piece, rows.at[pl.ds(i * each, each)], arrived.at[i])
        for i, piece in enumerate(pieces)
    ]
    for copy in copies:
        copy.start()
    swap_in.start()
    peaks[...] = jnp.zeros_like(peaks)
    for copy in copies:
        copy.wait()

    sources = (EARLY, CHIPS - EARLY)[part]
    tokens = rows.shape[1]
    each = out.shape[1]
    pairs = sources * each
    lanes = lists.shape[1]
    lower = lax.broadcasted_iota(jnp.int32, (1, 2 * tokens), 1) < tokens
    token = lax.broadcasted_iota(jnp.int32, (own.shape[1], LANE * tokens), 0)
    for which, texts in enumerate((own, theirs)):
        if which == 1:
            swap_in.wait()
        start = start_of(part, which) // lanes

        def step(i, carry):
            line = start + i * (UNROLL * LANE) // lanes
            first = i * (UNROLL * LANE) % lanes
            for u in range(UNROLL):
                code = [lists[line, first + u * LANE + k] for k in range(LANE)]
                passage = code[0] >> 20
                similar = lax.dot_general(
                    texts[passage],
                    jnp.concatenate([rows[(c >> 11) & 511] for c in code], axis=0),
                    (((1,), (1,)), ((), ())),
                    preferred_element_type=jnp.float32,
                )
                inside = token < lengths[which * own.shape[0] + passage]
                top = jnp.max(jnp.where(inside, similar, -jnp.inf), axis=0, keepdims=True)
                for k in range(0, LANE, 2):
                    both = top[:, k * tokens : (k + 2) * tokens]
                    peaks[pl.ds(code[k] & 2047, 1), :] = jnp.where(lower, both, 0.0)
                    peaks[pl.ds(code[k + 1] & 2047, 1), :] = jnp.where(lower, 0.0, both)
            return carry

        steps = (lists[lists.shape[0] - 8, part * 2 + which] + UNROLL - 1) // UNROLL
        lax.fori_loop(0, steps, step, 0)
    high = peaks[0:pairs, :].astype(jnp.bfloat16)
    low = (peaks[0:pairs, :] - high.astype(jnp.float32)).astype(jnp.bfloat16)
    ones = jnp.ones((16, 2 * tokens), jnp.bfloat16)
    total = sum(
        lax.dot_general(
            ones, part, (((1,), (1,)), ((), ())), preferred_element_type=jnp.float32
        )
        for part in (high, low)
    )
    total = total[0:1] * (1.0 / tokens)
    if before:
        out[...] = before[0][...]
    at, core = dict(zip("yxz", (here[0], here[1], here[2]))), here[3]
    for source in range(sources):
        third = (0, 1, 3)[source // (SIDE * SIDE)] if part == 0 else 2
        digits = (source % SIDE, source // SIDE % SIDE, third)
        chip = chip_low(at, by_core(core, digits))
        out[pl.ds(chip, 1), :] = total[:, source * each : (source + 1) * each]


def score(here, lists, lengths, pieces, own, sibling, before=()):
    pairs = CHIPS * 2 * SLOTS * CAPS
    many = len(pieces)
    tokens = pieces[0].shape[1]
    part = len(before)
    piece = pieces[0].shape
    scratch = [
        pltpu.VMEM((many * piece[0],) + piece[1:], own.dtype),
        pltpu.VMEM(sibling.shape, sibling.dtype),
        pltpu.SemaphoreType.DMA((many + 1,)),
        pltpu.VMEM((NOBODY + 8, 2 * tokens), jnp.float32),
    ]
    return pl.pallas_call(
        lambda *refs: score_kernel(part, many, *refs),
        out_shape=jax.ShapeDtypeStruct((CHIPS, pairs // CHIPS), jnp.float32),
        in_specs=[smem()] * 3
        + [hbm()] * many
        + [vmem(), hbm()]
        + [vmem()] * len(before),
        out_specs=vmem(),
        scratch_shapes=scratch,
        cost_estimate=cost(8 if before else 12),
        compiler_params=pltpu.CompilerParams(vmem_limit_bytes=(26 if before else 56) * MIB),
    )(here, lists, lengths, *pieces, own, sibling, *before)


def of_owner(here, which):
    chip = lax.broadcasted_iota(jnp.int32, (CHIPS, 2 * CHIPS), 0)
    device = lax.broadcasted_iota(jnp.int32, (CHIPS, 2 * CHIPS), 1)
    core = here[3] if which == 0 else 1 - here[3]
    return jnp.where(device == chip * 2 + core, 1.0, 0.0)


def used_caps(send_count, cand_count):
    slot = lax.broadcasted_iota(jnp.int32, cand_count.shape, 0)
    return jnp.where(slot < send_count, cand_count, 0)


def tell_kernel(here, send_count, cand_count, cand, out):
    used = used_caps(send_count[...], cand_count[...]).astype(jnp.float32)
    rest = jnp.zeros((NOTES - used.shape[0] - cand.shape[0], used.shape[1]), jnp.float32)
    told = jnp.concatenate([used, cand[...].astype(jnp.float32), rest], axis=0)
    told = told.astype(jnp.bfloat16)
    out[...] = jnp.zeros_like(out)
    for which in range(2):
        note = lax.dot_general(
            of_owner(here, which).astype(jnp.bfloat16),
            told,
            (((1,), (1,)), ((), ())),
            preferred_element_type=jnp.float32,
        )
        out[:, which * NOTES : (which + 1) * NOTES] = note.astype(jnp.int32)


def tell(here, send_count, cand_count, cand, after):
    return pl.pallas_call(
        lambda here, after, *refs: tell_kernel(here, *refs),
        out_shape=jax.ShapeDtypeStruct((CHIPS, 128), jnp.int32),
        in_specs=[smem(), hbm(), vmem(), vmem(), vmem()],
        out_specs=vmem(),
        cost_estimate=cost(1),
    )(here, after, send_count, cand_count, cand)


def finish_kernel(here, returned, send_count, cand_count, conts, scores, best):
    each = SLOTS * CAPS
    values = sum(
        lax.dot_general(
            returned[:, which * each : (which + 1) * each],
            of_owner(here, which),
            (((0,), (0,)), ((), ())),
            precision=lax.Precision.HIGHEST,
            preferred_element_type=jnp.float32,
        )
        for which in range(2)
    )
    used = used_caps(send_count[...], cand_count[...])
    lanes = values.shape[1]
    cap = lax.broadcasted_iota(jnp.int32, (CAPS, lanes), 0)
    cont = lax.broadcasted_iota(jnp.int32, (CONTS, lanes), 0)
    tops = jnp.full((CONTS, lanes), -jnp.inf, jnp.float32)
    for j in range(SLOTS):
        value = values[j * CAPS : (j + 1) * CAPS]
        live = cap < used[j : j + 1]
        scores[j * CAPS : (j + 1) * CAPS, :] = jnp.where(live, value, 0.0)
        top = jnp.max(jnp.where(live, value, -jnp.inf), axis=0, keepdims=True)
        tops = jnp.maximum(tops, jnp.where(conts[j : j + 1, :] == cont, top, -jnp.inf))
    top = jnp.max(tops, axis=1, keepdims=True)
    top = jnp.where(top > -jnp.inf, top, 0.0)
    best[...] = jnp.broadcast_to(top, (CONTS, lanes)).T[0:1]


def finish(here, returned, send_count, cand_count, conts):
    devices = 2 * CHIPS
    return pl.pallas_call(
        finish_kernel,
        out_shape=(
            jax.ShapeDtypeStruct((SLOTS * CAPS, devices), jnp.float32),
            jax.ShapeDtypeStruct((1, CONTS), jnp.float32),
        ),
        in_specs=[smem()] + [vmem()] * 4,
        out_specs=(vmem(), vmem()),
        cost_estimate=cost(2),
    )(here, returned, send_count, cand_count, conts)


def body(queries, passages, pass_len, send_cont, send_count, cand, cand_count):
    here = jnp.stack([lax.axis_index(k) for k in ALL]).astype(jnp.int32)
    conts = send_cont[0].T
    counts = cand_count[0].T
    chosen = cand[0].transpose(1, 2, 0).reshape(SLOTS * CAPS, -1)

    told = jnp.pad(conts.astype(queries.dtype), ((0, NOTE_ROWS - SLOTS), (0, 0)))
    piece = jnp.concatenate([queries.reshape(-1, queries.shape[2]), told], axis=0)
    line = jnp.stack([piece] + [shift(piece, 0, by) for by in range(1, SIDE)])
    planes = [line] + [shift(line, 1, by) for by in range(1, SIDE)]
    notes = tell(here, send_count, counts, chosen, line)
    notes = lax.all_to_all(notes, PLACE, split_axis=0, concat_axis=0, tiled=True)

    swap = [(0, 1), (1, 0)]
    sibling = lax.ppermute(passages, "core", swap)
    lengths = jnp.concatenate([pass_len, lax.ppermute(pass_len, "core", swap)])

    halves = [
        select(range(SIDE), here, here, planes[:2]),
        select(range(SIDE), here, notes, planes[2:]),
    ]
    near = [shift(half[1], 2, 1) for half in halves]
    back = [shift(half[3], 2, 3) for half in halves]
    lists, across = group_pairs(here, notes, halves[1][2])
    far = [shift(halves[0][2], 2, 2), shift(across, 2, 2)]
    around = [half[0] for half in halves] + near + back
    handled = score(here, lists, lengths, around, passages, sibling)
    handled = score(here, lists, lengths, far, passages, sibling, (handled,))
    returned = lax.all_to_all(handled, PLACE, split_axis=0, concat_axis=0, tiled=True)
    scores, best = finish(here, returned, send_count, counts, conts)
    scores = scores.reshape(1, SLOTS, CAPS, -1).transpose(0, 3, 1, 2)
    return scores, best.reshape(-1)


def solution(mesh):
    mesh = Mesh(mesh.devices.reshape(SIDE, SIDE, SIDE, 2), ALL)
    in_specs = (
        P(ALL, None, None),
        P(ALL, None, None),
        P(ALL),
        P(ALL, None, None),
        P(ALL, None),
        P(ALL, None, None, None),
        P(ALL, None, None),
    )
    out_specs = (P(ALL, None, None, None), P(ALL))
    return jax.shard_map(body, mesh=mesh, in_specs=in_specs, out_specs=out_specs, check_vma=False)
```

```python
import itertools

import jax
import jax.numpy as jnp
from jax import lax
from jax.experimental import pallas as pl
from jax.experimental.pallas import tpu as pltpu
from jax.sharding import Mesh, PartitionSpec as P

ALL = ("y", "x", "z", "core")
PLACE = ("y", "x", "z")
SIDE = 4
CHIPS = SIDE**3
EARLY = CHIPS * 3 // 4
CAPS = 4
SLOTS = 4
LANE = 4
UNROLL = 32
NOBODY = EARLY * 2 * SLOTS * CAPS
MIB = 1 << 20
CONTS = 16
NOTE_ROWS = 16
NOTES = 32
PASSAGES = 128

ORDERS = (("x", "y", "z"), ("y", "z", "x"))


def smem():
    return pl.BlockSpec(memory_space=pltpu.SMEM)


def vmem():
    return pl.BlockSpec(memory_space=pltpu.VMEM)


def hbm():
    return pl.BlockSpec(memory_space=pl.ANY)


def shift(array, stage, by):
    pairs = []
    for y, x, z, core in itertools.product(range(SIDE), range(SIDE), range(SIDE), range(2)):
        at = {"y": y, "x": x, "z": z}
        axis = ORDERS[core][stage]
        to = dict(at, **{axis: (at[axis] + by) % SIDE})
        pairs.append(tuple(((p["y"] * SIDE + p["x"]) * SIDE + p["z"]) * 2 + core for p in (at, to)))
    return lax.ppermute(array, ALL, pairs)


def cost(us):
    return pl.CostEstimate(flops=0, bytes_accessed=int(us * 3_500_000), transcendentals=0)


def chip_low(at, low):
    y, x, z = ((at[k] - low[k]) & (SIDE - 1) for k in "yxz")
    return (y * SIDE + x) * SIDE + z


def by_core(core, digits):
    low = [dict(zip(order, digits)) for order in ORDERS]
    return {k: jnp.where(core == 0, low[0][k], low[1][k]) for k in "yxz"}


def select_kernel(targets, here, after, *refs):
    *planes, table, notes, arrived = refs
    planes, outs = planes[: -len(targets)], planes[-len(targets) :]
    at, core = dict(zip("yxz", (here[0], here[1], here[2]))), here[3]
    end = planes[0].shape[1] - NOTE_ROWS
    tokens = end // CONTS
    for source in range(SIDE * len(planes)):
        told = planes[source // SIDE][source % SIDE, end : end + NOTE_ROWS, :]
        table[source] = told.astype(jnp.float32).astype(jnp.int32)[:8]
    copy = pltpu.make_async_copy(table, notes, arrived)
    copy.start()
    owners = []
    for third in targets:
        chip = chip_low(at, by_core(core, (0, 0, -third)))
        owners += [chip * 2 + core, chip * 2 + 1 - core]
    copy.wait()
    for second in range(len(planes)):

        def step(first, carry):
            source = second * SIDE + first
            for out, target in enumerate(outs):
                picked = []
                for slot in range(2 * SLOTS):
                    cont = notes[source, slot % SLOTS, owners[out * 2 + slot // SLOTS]]
                    rows = pl.ds(pl.multiple_of(cont * tokens, 16), tokens)
                    picked.append(planes[second][first, rows, :])
                for slot, rows in enumerate(picked):
                    target[source * 2 * SLOTS + slot] = rows
            return carry

        lax.fori_loop(0, SIDE, step, 0)


def select(targets, here, after, planes):
    tokens = (planes[0].shape[1] - NOTE_ROWS) // CONTS
    sources = SIDE * len(planes)
    shape = (sources * 2 * SLOTS, tokens, planes[0].shape[2])
    return pl.pallas_call(
        lambda *refs: select_kernel(targets, *refs),
        out_shape=[jax.ShapeDtypeStruct(shape, planes[0].dtype)] * len(targets),
        in_specs=[smem(), hbm()] + [vmem()] * len(planes),
        out_specs=[vmem()] * len(targets),
        cost_estimate=cost(4),
        scratch_shapes=[
            pltpu.VMEM((sources, 8, 128), jnp.int32),
            pltpu.SMEM((sources, 8, 128), jnp.int32),
            pltpu.SemaphoreType.DMA(()),
        ],
        compiler_params=pltpu.CompilerParams(vmem_limit_bytes=14 * MIB),
    )(here, after, *planes)


def room(part):
    sources = (EARLY, CHIPS - EARLY)[part]
    most = (sources * SLOTS * CAPS + (LANE - 1) * PASSAGES) // LANE
    return -(-most // 32) * 32


def start_of(part, which):
    before = 2 * sum(room(p) for p in range(part))
    return (before + (room(part) * which if which else 0)) * LANE


def group_kernel(here, notes, held, lists, passed, blank, table, spots, arrived):
    rows, lanes = lists.shape
    counts_row = rows - 8
    dump = counts_row * lanes + lanes // 2
    core = here[3]
    source = lax.broadcasted_iota(jnp.int32, (CHIPS, 1), 0)
    far_y = (here[0] - (source >> 4)) & (SIDE - 1)
    far_x = (here[1] - (source >> 2)) & (SIDE - 1)
    far_z = (here[2] - source) & (SIDE - 1)
    first = jnp.where(core == 0, far_x, far_y)
    second = jnp.where(core == 0, far_y, far_z)
    third = jnp.where(core == 0, far_z, far_x)
    late = third == 2
    third = jnp.where(late, 0, jnp.where(third == 3, 2, third))
    local = (third * SIDE + second) * SIDE + first
    shift_late = jnp.where(late, PASSAGES, 0)

    lane = lax.broadcasted_iota(jnp.int32, (CHIPS, lanes), 1)
    key = lax.broadcasted_iota(jnp.int32, (CHIPS, 2 * PASSAGES), 1)
    square = (CHIPS, CHIPS)
    earlier = lax.broadcasted_iota(jnp.int32, square, 1) < lax.broadcasted_iota(jnp.int32, square, 0)
    earlier = earlier.astype(jnp.float32).astype(jnp.bfloat16)
    square = (PASSAGES, PASSAGES)
    below = lax.broadcasted_iota(jnp.int32, square, 0) < lax.broadcasted_iota(jnp.int32, square, 1)
    below = below.astype(jnp.float32).astype(jnp.bfloat16)
    data = notes[...]
    found = jnp.zeros((CHIPS, lanes), jnp.int32)
    counts = jnp.zeros((1, lanes), jnp.int32)
    lane_row = lax.broadcasted_iota(jnp.int32, (1, lanes), 1)

    for which in range(2):
        info = which * NOTES
        hits, ranks, lives = [], [], []
        many = jnp.zeros((1, 2 * PASSAGES), jnp.float32)
        for j in range(SLOTS):
            for k in range(CAPS):
                at = info + SLOTS + j * CAPS + k
                passage = data[:, at : at + 1]
                live = data[:, info + j : info + j + 1] > k
                hit = jnp.where(live & (passage + shift_late == key), 1.0, 0.0)
                ahead = jnp.dot(
                    earlier, hit.astype(jnp.bfloat16), preferred_element_type=jnp.float32
                )
                ranks.append(jnp.sum(hit * (ahead + many), axis=1, keepdims=True))
                many = many + jnp.sum(hit, axis=0, keepdims=True)
                hits.append(hit)
                lives.append(live)
                slot = local * (2 * SLOTS) + which * SLOTS + j
                code = (passage << 20) | (slot << 11) | (slot * CAPS + k)
                pair = (which * SLOTS + j) * CAPS + k
                found = jnp.where(lane == 32 + pair, code, found)
        groups = (many.astype(jnp.int32) + (LANE - 1)) // LANE
        starts = []
        for part in range(2):
            mine = groups[:, part * PASSAGES : (part + 1) * PASSAGES]
            wide = jnp.broadcast_to(mine.astype(jnp.float32), (16, PASSAGES)).astype(jnp.bfloat16)
            base = jnp.dot(wide, below, preferred_element_type=jnp.float32)[0:1]
            starts.append(base * LANE + start_of(part, which))
            total = jnp.sum(mine.astype(jnp.float32), axis=1, keepdims=True).astype(jnp.int32)
            counts = jnp.where(lane_row == part * 2 + which, total, counts)
        begin = jnp.concatenate(starts, axis=1)
        for i, (hit, rank, live) in enumerate(zip(hits, ranks, lives)):
            spot = jnp.sum(hit * begin, axis=1, keepdims=True) + rank
            spot = jnp.where(live, spot.astype(jnp.int32), dump)
            found = jnp.where(lane == which * SLOTS * CAPS + i, spot, found)

    table[...] = found
    blank[...] = jnp.full((rows, lanes), NOBODY, jnp.int32)
    blank[counts_row : counts_row + 1, :] = counts
    copies = [
        pltpu.make_async_copy(table, spots, arrived.at[0]),
        pltpu.make_async_copy(blank, lists, arrived.at[1]),
    ]
    for copy in copies:
        copy.start()
    for copy in copies:
        copy.wait()

    def scatter(source, carry):
        for pair in range(2 * SLOTS * CAPS):
            spot = spots[source, pair]
            lists[spot >> 7, spot & 127] = spots[source, 32 + pair]
        return carry

    lax.fori_loop(0, CHIPS, scatter, 0)


def group_pairs(here, notes, held):
    rows = start_of(2, 0) // 128 + 8
    rows = -(-rows // 8) * 8
    return pl.pallas_call(
        group_kernel,
        out_shape=(
            jax.ShapeDtypeStruct((rows, 128), jnp.int32),
            jax.ShapeDtypeStruct(held.shape, held.dtype),
        ),
        in_specs=[smem(), vmem(), hbm()],
        out_specs=(smem(), hbm()),
        input_output_aliases={2: 1},
        scratch_shapes=[
            pltpu.VMEM((rows, 128), jnp.int32),
            pltpu.VMEM((CHIPS, 128), jnp.int32),
            pltpu.SMEM((CHIPS, 128), jnp.int32),
            pltpu.SemaphoreType.DMA((2,)),
        ],
        cost_estimate=cost(8),
        compiler_params=pltpu.CompilerParams(vmem_limit_bytes=16 * MIB),
    )(here, notes, held)


def score_kernel(part, many, here, lists, lengths, *refs):
    pieces, refs = refs[:many], refs[many:]
    own, sibling, refs = refs[0], refs[1], refs[2:]
    *refs, theirs, arrived, peaks = refs
    swap_in = pltpu.make_async_copy(sibling, theirs, arrived.at[many])
    *before, out, rows = refs
    each = pieces[0].shape[0]
    copies = [
        pltpu.make_async_copy(piece, rows.at[pl.ds(i * each, each)], arrived.at[i])
        for i, piece in enumerate(pieces)
    ]
    for copy in copies:
        copy.start()
    swap_in.start()
    peaks[...] = jnp.zeros_like(peaks)
    for copy in copies:
        copy.wait()

    sources = (EARLY, CHIPS - EARLY)[part]
    tokens = rows.shape[1]
    each = out.shape[1]
    pairs = sources * each
    lanes = lists.shape[1]
    lower = lax.broadcasted_iota(jnp.int32, (1, 2 * tokens), 1) < tokens
    token = lax.broadcasted_iota(jnp.int32, (own.shape[1], LANE * tokens), 0)
    for which, texts in enumerate((own, theirs)):
        if which == 1:
            swap_in.wait()
        start = start_of(part, which) // lanes

        def step(i, carry):
            line = start + i * (UNROLL * LANE) // lanes
            first = i * (UNROLL * LANE) % lanes
            for u in range(UNROLL):
                code = [lists[line, first + u * LANE + k] for k in range(LANE)]
                passage = code[0] >> 20
                similar = lax.dot_general(
                    texts[passage],
                    jnp.concatenate([rows[(c >> 11) & 511] for c in code], axis=0),
                    (((1,), (1,)), ((), ())),
                    preferred_element_type=jnp.float32,
                )
                inside = token < lengths[which * own.shape[0] + passage]
                top = jnp.max(jnp.where(inside, similar, -jnp.inf), axis=0, keepdims=True)
                for k in range(0, LANE, 2):
                    both = top[:, k * tokens : (k + 2) * tokens]
                    peaks[pl.ds(code[k] & 2047, 1), :] = jnp.where(lower, both, 0.0)
                    peaks[pl.ds(code[k + 1] & 2047, 1), :] = jnp.where(lower, 0.0, both)
            return carry

        steps = (lists[lists.shape[0] - 8, part * 2 + which] + UNROLL - 1) // UNROLL
        lax.fori_loop(0, steps, step, 0)
    high = peaks[0:pairs, :].astype(jnp.bfloat16)
    low = (peaks[0:pairs, :] - high.astype(jnp.float32)).astype(jnp.bfloat16)
    ones = jnp.ones((16, 2 * tokens), jnp.bfloat16)
    total = sum(
        lax.dot_general(
            ones, part, (((1,), (1,)), ((), ())), preferred_element_type=jnp.float32
        )
        for part in (high, low)
    )
    total = total[0:1] * (1.0 / tokens)
    if before:
        out[...] = before[0][...]
    at, core = dict(zip("yxz", (here[0], here[1], here[2]))), here[3]
    for source in range(sources):
        third = (0, 1, 3)[source // (SIDE * SIDE)] if part == 0 else 2
        digits = (source % SIDE, source // SIDE % SIDE, third)
        chip = chip_low(at, by_core(core, digits))
        out[pl.ds(chip, 1), :] = total[:, source * each : (source + 1) * each]


def score(here, lists, lengths, pieces, own, sibling, before=()):
    pairs = CHIPS * 2 * SLOTS * CAPS
    many = len(pieces)
    tokens = pieces[0].shape[1]
    part = len(before)
    piece = pieces[0].shape
    scratch = [
        pltpu.VMEM((many * piece[0],) + piece[1:], own.dtype),
        pltpu.VMEM(sibling.shape, sibling.dtype),
        pltpu.SemaphoreType.DMA((many + 1,)),
        pltpu.VMEM((NOBODY + 8, 2 * tokens), jnp.float32),
    ]
    return pl.pallas_call(
        lambda *refs: score_kernel(part, many, *refs),
        out_shape=jax.ShapeDtypeStruct((CHIPS, pairs // CHIPS), jnp.float32),
        in_specs=[smem()] * 3
        + [hbm()] * many
        + [vmem(), hbm()]
        + [vmem()] * len(before),
        out_specs=vmem(),
        scratch_shapes=scratch,
        cost_estimate=cost(8 if before else 12),
        compiler_params=pltpu.CompilerParams(vmem_limit_bytes=(26 if before else 56) * MIB),
    )(here, lists, lengths, *pieces, own, sibling, *before)


def of_owner(here, which):
    chip = lax.broadcasted_iota(jnp.int32, (CHIPS, 2 * CHIPS), 0)
    device = lax.broadcasted_iota(jnp.int32, (CHIPS, 2 * CHIPS), 1)
    core = here[3] if which == 0 else 1 - here[3]
    return jnp.where(device == chip * 2 + core, 1.0, 0.0)


def used_caps(send_count, cand_count):
    slot = lax.broadcasted_iota(jnp.int32, cand_count.shape, 0)
    return jnp.where(slot < send_count, cand_count, 0)


def tell_kernel(here, send_count, cand_count, cand, out):
    used = used_caps(send_count[...], cand_count[...]).astype(jnp.float32)
    rest = jnp.zeros((NOTES - used.shape[0] - cand.shape[0], used.shape[1]), jnp.float32)
    told = jnp.concatenate([used, cand[...].astype(jnp.float32), rest], axis=0)
    told = told.astype(jnp.bfloat16)
    out[...] = jnp.zeros_like(out)
    for which in range(2):
        note = lax.dot_general(
            of_owner(here, which).astype(jnp.bfloat16),
            told,
            (((1,), (1,)), ((), ())),
            preferred_element_type=jnp.float32,
        )
        out[:, which * NOTES : (which + 1) * NOTES] = note.astype(jnp.int32)


def tell(here, send_count, cand_count, cand, after):
    return pl.pallas_call(
        lambda here, after, *refs: tell_kernel(here, *refs),
        out_shape=jax.ShapeDtypeStruct((CHIPS, 128), jnp.int32),
        in_specs=[smem(), hbm(), vmem(), vmem(), vmem()],
        out_specs=vmem(),
        cost_estimate=cost(1),
    )(here, after, send_count, cand_count, cand)


def finish_kernel(here, returned, send_count, cand_count, conts, scores, best):
    each = SLOTS * CAPS
    values = sum(
        lax.dot_general(
            returned[:, which * each : (which + 1) * each],
            of_owner(here, which),
            (((0,), (0,)), ((), ())),
            precision=lax.Precision.HIGHEST,
            preferred_element_type=jnp.float32,
        )
        for which in range(2)
    )
    used = used_caps(send_count[...], cand_count[...])
    lanes = values.shape[1]
    cap = lax.broadcasted_iota(jnp.int32, (CAPS, lanes), 0)
    cont = lax.broadcasted_iota(jnp.int32, (CONTS, lanes), 0)
    tops = jnp.full((CONTS, lanes), -jnp.inf, jnp.float32)
    for j in range(SLOTS):
        value = values[j * CAPS : (j + 1) * CAPS]
        live = cap < used[j : j + 1]
        scores[j * CAPS : (j + 1) * CAPS, :] = jnp.where(live, value, 0.0)
        top = jnp.max(jnp.where(live, value, -jnp.inf), axis=0, keepdims=True)
        tops = jnp.maximum(tops, jnp.where(conts[j : j + 1, :] == cont, top, -jnp.inf))
    top = jnp.max(tops, axis=1, keepdims=True)
    top = jnp.where(top > -jnp.inf, top, 0.0)
    best[...] = jnp.broadcast_to(top, (CONTS, lanes)).T[0:1]


def finish(here, returned, send_count, cand_count, conts):
    devices = 2 * CHIPS
    return pl.pallas_call(
        finish_kernel,
        out_shape=(
            jax.ShapeDtypeStruct((SLOTS * CAPS, devices), jnp.float32),
            jax.ShapeDtypeStruct((1, CONTS), jnp.float32),
        ),
        in_specs=[smem()] + [vmem()] * 4,
        out_specs=(vmem(), vmem()),
        cost_estimate=cost(2),
    )(here, returned, send_count, cand_count, conts)


def body(queries, passages, pass_len, send_cont, send_count, cand, cand_count):
    here = jnp.stack([lax.axis_index(k) for k in ALL]).astype(jnp.int32)
    conts = send_cont[0].T
    counts = cand_count[0].T
    chosen = cand[0].transpose(1, 2, 0).reshape(SLOTS * CAPS, -1)

    told = jnp.pad(conts.astype(queries.dtype), ((0, NOTE_ROWS - SLOTS), (0, 0)))
    piece = jnp.concatenate([queries.reshape(-1, queries.shape[2]), told], axis=0)
    line = jnp.stack([piece] + [shift(piece, 0, by) for by in range(1, SIDE)])
    planes = [line] + [shift(line, 1, by) for by in range(1, SIDE)]
    notes = tell(here, send_count, counts, chosen, line)
    notes = lax.all_to_all(notes, PLACE, split_axis=0, concat_axis=0, tiled=True)

    swap = [(0, 1), (1, 0)]
    sibling = lax.ppermute(passages, "core", swap)
    lengths = jnp.concatenate([pass_len, lax.ppermute(pass_len, "core", swap)])

    halves = [
        select(range(SIDE), here, here, planes[:2]),
        select(range(SIDE), here, notes, planes[2:]),
    ]
    near = [shift(half[1], 2, 1) for half in halves]
    back = [shift(half[3], 2, 3) for half in halves]
    lists, across = group_pairs(here, notes, halves[1][2])
    far = [shift(halves[0][2], 2, 2), shift(across, 2, 2)]
    around = [half[0] for half in halves] + near + back
    handled = score(here, lists, lengths, around, passages, sibling)
    handled = score(here, lists, lengths, far, passages, sibling, (handled,))
    returned = lax.all_to_all(handled, PLACE, split_axis=0, concat_axis=0, tiled=True)
    scores, best = finish(here, returned, send_count, counts, conts)
    scores = scores.reshape(1, SLOTS, CAPS, -1).transpose(0, 3, 1, 2)
    return scores, best.reshape(-1)


def solution(mesh):
    mesh = Mesh(mesh.devices.reshape(SIDE, SIDE, SIDE, 2), ALL)
    in_specs = (
        P(ALL, None, None),
        P(ALL, None, None),
        P(ALL),
        P(ALL, None, None),
        P(ALL, None),
        P(ALL, None, None, None),
        P(ALL, None, None),
    )
    out_specs = (P(ALL, None, None, None), P(ALL))
    return jax.shard_map(body, mesh=mesh, in_specs=in_specs, out_specs=out_specs, check_vma=False)
```
